512 devices in a mesh: frame: 32 (over x, z_lo, core), batch: 16 (over z_hi, y).
Axes of the slice: x: 4, y: 8, z: 8 (z_hi: 2, z_lo: 4; z = z_hi * 4 + z_lo), core: 2. Of those that a mesh axis runs over, the one named last changes fastest.
Arguments:
- window: float32 [262144, 128], P(('batch', 'frame')), parts along dimension 0, may hold values from -6 to 6
- noise: float32 [262144, 2, 128], P(('batch', 'frame')), parts along dimension 0, may hold values from -6 to 6
- fresh: float32 [8192, 128], P('batch'), parts along dimension 0, may hold values from -12 to 12
- levels: int32 [512, 2], P(('batch', 'frame')), parts along dimension 0, may hold values from 0 to 31
- reach: int32 [512], P('batch'), parts along dimension 0, may hold values from 1 to 31
- w_in: bfloat16 [128, 1024], replicated, may hold values from -0.5 to 0.5
- w_level: bfloat16 [256, 1024], replicated, may hold values from -0.375 to 0.375
- norm_gain: float32 [1024], replicated, may hold values from 0.25 to 1.75
- w_qkv: bfloat16 [1024, 3072], P('frame'), as said below
- w_out: bfloat16 [1024, 128], replicated, may hold values from -0.1875 to 0.1875
- w_res: bfloat16 [1024, 128], replicated, may hold values from -0.1875 to 0.1875
Outputs:
- final_window: float32 [262144, 128], P(('batch', 'frame')), parts along dimension 0
The draws below stay inside these ranges and needn't reach their ends.
There are 16 independent parts, one for each index of `batch`. The reference program is written for one: setup_inputs(seed, part) draws one part's arguments, and reference() takes and returns one part's arrays. A program takes and returns all parts, laid end to end along the dimension named above; an argument that names none is the same for every part. Nothing has to cross between parts.
Inputs may be any that keep to these rules, and one draw needn't show every extreme that they name: `w_qkv`: projection weights of fan-in 1024.
All inputs are finite; a program needn't handle non-finite values.
Results may differ from the reference program's by a relative error of at most 0.017.
Values may be sent and summed in bfloat16 or wider, within the bound.
No kernel may reach another device: no remote copies, remote signals or barrier semaphores. Data moves between devices by JAX's collectives and lax.ppermute only.
A program may use at most 64 MiB of HBM per device.

```python
import math
import jax
import jax.numpy as jnp
from jax import lax

D = 1024
HEADS = 8
HDIM = 128
C = 128
FREQ = 128
ROWS = 512
PASSES = 2
LEVELS = 32
WIN = 16384
N_FRAME = 32


def draw_w_qkv(key, part):
    key = jax.random.fold_in(key, 7)
    key_base = jax.random.fold_in(key, 0)
    width = HEADS * HDIM
    base = jax.random.normal(key_base, (D, 3 * width), jnp.float32) * D ** (-0.5)
    return base.astype(jnp.bfloat16)


def touch_ends(drawn, own_key, smallest, top_value):
    place = [jax.random.randint(jax.random.fold_in(own_key, axis), (), 0, length) for axis, length in enumerate(drawn.shape)]
    longest = drawn.shape.index(max(drawn.shape))
    beside = place[:longest] + [(place[longest] + 1) % drawn.shape[longest]] + place[longest + 1:]
    return drawn.at[tuple(place)].set(smallest).at[tuple(beside)].set(top_value)


def level_of(stream_key, shape, cuts, smallest, top_value):
    gain = 1.0
    for position, shards_of in cuts:
        draws = jax.random.uniform(jax.random.fold_in(jax.random.fold_in(stream_key, 6), position), (shards_of,), jnp.float32, smallest / len(cuts), top_value / len(cuts))
        gain = gain * jnp.repeat(jnp.exp(draws), shape[position] // shards_of).reshape((-1,) + (1,) * (len(shape) - 1 - position))
    return gain


def gaussian(key, shape, scale, limit, shards=(), kind=jnp.bfloat16):
    level = level_of(key, shape, shards, -0.22, 0.18) if shards else 1.0
    values = jax.random.normal(key, shape, jnp.float32) * scale * level
    return jnp.minimum(jnp.maximum(values, -limit), limit).astype(kind)


def setup_inputs(seed: int = 0, part: int = 0) -> dict:
    arg_keys = jax.random.split(jax.random.key(seed), 12)
    part_keys = jax.random.split(jax.random.fold_in(arg_keys[11], part), 12)
    return {
        "window": gaussian(part_keys[0], (WIN, C), 1.0, 6.0, ((0, 32),), jnp.float32),
        "noise": gaussian(part_keys[1], (WIN, PASSES, C), 1.0, 6.0, ((0, 32),), jnp.float32),
        "fresh": gaussian(part_keys[2], ((PASSES - 1) * ROWS, C), 2.0, 12.0, (), jnp.float32),
        "levels": touch_ends(jax.random.randint(part_keys[3], (N_FRAME, PASSES), 0, LEVELS), jax.random.fold_in(part_keys[3], 1), 0, LEVELS - 1).astype(jnp.int32),
        "reach": touch_ends(jax.random.randint(part_keys[4], (N_FRAME,), 1, N_FRAME), jax.random.fold_in(part_keys[4], 1), 1, N_FRAME - 1).astype(jnp.int32),
        "w_in": gaussian(arg_keys[5], (C, D), C ** -0.5, 0.5),
        "w_level": gaussian(arg_keys[6], (2 * FREQ, D), (2 * FREQ) ** -0.5, 0.375),
        "norm_gain": jnp.clip(1.0 + 0.15 * jax.random.normal(arg_keys[7], (D,), jnp.float32), 0.25, 1.75),
        "w_qkv": draw_w_qkv(jax.random.fold_in(arg_keys[11], 71), part),
        "w_out": gaussian(arg_keys[9], (HEADS * HDIM, C), (HEADS * HDIM) ** -0.5, 0.1875),
        "w_res": gaussian(arg_keys[10], (D, C), D ** -0.5, 0.1875),
    }


def sigma_of(level):
    return 4.0 * jnp.exp(level.astype(jnp.float32) * jnp.float32(math.log(1.0 / 16.0) / LEVELS))

def level_feats(level):
    sigma = sigma_of(level)
    index = jnp.arange(FREQ).astype(jnp.float32)
    freqs = jnp.exp(index * jnp.float32(math.log(100.0) / FREQ))
    angle = jnp.log(sigma)[:, None] * freqs[None, :]
    return jnp.concatenate([jnp.sin(angle), jnp.cos(angle)], axis=1).astype(jnp.bfloat16)

def one_pass(state, levels_now, noise_now, reach, w_in, w_level, norm_gain, w_qkv, w_out, w_res):
    frames = state.shape[0]
    sigma = sigma_of(levels_now)[:, None, None]
    sigma_next = sigma_of(levels_now + 1)[:, None, None]
    scaled = (state / jnp.sqrt(1.0 + sigma * sigma)).astype(jnp.bfloat16)
    embed = jnp.dot(level_feats(levels_now), w_level, preferred_element_type=jnp.float32)
    hidden = jnp.dot(scaled.reshape(-1, C), w_in, preferred_element_type=jnp.float32).reshape(frames, ROWS, D)
    hidden = hidden + embed[:, None, :]
    normed = hidden * jax.lax.rsqrt(lax.optimization_barrier(jnp.mean(hidden * hidden, axis=-1, keepdims=True)) + 1e-06) * norm_gain
    normed = normed.astype(jnp.bfloat16)
    qkv = jnp.dot(normed.reshape(-1, D), w_qkv, preferred_element_type=jnp.float32).astype(jnp.bfloat16)
    qkv = qkv.reshape(frames, ROWS, 3, HEADS, HDIM).astype(jnp.float32)
    query, keys, values = (qkv[:, :, 0], qkv[:, :, 1], qkv[:, :, 2])
    scores = jnp.einsum('fnhd,gnhd->nhfg', query, keys) / jnp.float32(math.sqrt(HDIM))
    slots = jnp.arange(frames).astype(jnp.int32)
    allowed = (slots[None, :] <= slots[:, None]) & (slots[None, :] >= slots[:, None] - reach[:, None])
    scores = jnp.where(allowed[None, None], scores, jnp.float32(-1e+30))
    top = lax.optimization_barrier(jnp.max(scores, axis=-1, keepdims=True))
    expo = jnp.exp(scores - top)
    probs = (expo / lax.optimization_barrier(jnp.sum(expo, axis=-1, keepdims=True))).astype(jnp.bfloat16)
    attn = jnp.einsum('nhfg,gnhd->fnhd', probs.astype(jnp.float32), values).astype(jnp.bfloat16)
    attn = attn.reshape(-1, HEADS * HDIM)
    pred = jnp.dot(attn, w_out, preferred_element_type=jnp.float32) + jnp.dot(normed.reshape(-1, D), w_res, preferred_element_type=jnp.float32)
    pred = pred.reshape(frames, ROWS, C)
    return state - sigma * pred + sigma_next * (0.8 * pred + 0.6 * noise_now)

def reference(window, noise, fresh, levels, reach, w_in, w_level, norm_gain, w_qkv, w_out, w_res):
    frames = window.shape[0] // ROWS
    state = window.reshape(frames, ROWS, C)
    noise_all = noise.reshape(frames, ROWS, PASSES, C)
    for step in range(PASSES):
        state = one_pass(state, levels[:, step], noise_all[:, :, step, :], reach, w_in, w_level, norm_gain, w_qkv, w_out, w_res)
        if step + 1 < PASSES:
            entering = fresh[step * ROWS:(step + 1) * ROWS][None]
            state = jnp.concatenate([state[1:], entering], axis=0)
    return state.reshape(-1, C)
```

```python
import math

import jax
import jax.numpy as jnp
import numpy as np
from jax import lax
from jax.experimental import pallas as pl
from jax.experimental.pallas import tpu as pltpu
from jax.sharding import PartitionSpec as P

HEADS = 8
HDIM = 128
C = 128
D = 1024
FREQ = 128
LEVELS = 32
FRAMES = 32
ROWS = 512
POS = ROWS // FRAMES
GROUP = 8
SPAN = FRAMES * GROUP
PART = 32
DECAY = math.log(1.0 / 16.0) / LEVELS
BF16 = jnp.bfloat16
F32 = jnp.float32
VMEM = pl.BlockSpec(memory_space=pltpu.VMEM)
SMEM = pl.BlockSpec(memory_space=pltpu.SMEM)


def sigma_of(level):
    return 4.0 * jnp.exp(level * F32(DECAY))


def feats_table():
    sigma = 4.0 * np.exp(np.arange(LEVELS) * DECAY)
    freqs = np.exp(np.arange(FREQ) * (math.log(100.0) / FREQ))
    angle = np.log(sigma)[:, None] * freqs[None, :]
    return jnp.asarray(np.concatenate([np.sin(angle), np.cos(angle)], axis=1), F32).astype(BF16)


def dot(a, b):
    return jnp.dot(a, b, preferred_element_type=F32)


def iota(shape, dim):
    return lax.broadcasted_iota(jnp.int32, shape, dim)


def pack_kernel(levels, window, noise, w_qkv, out, base_out, late_out):
    first = jnp.full((8, C), levels[0, 0], jnp.int32).astype(F32)
    second = jnp.full((8, C), levels[0, 1], jnp.int32).astype(F32)
    sigma = sigma_of(first)[:1]
    state = window[...]
    scaled = state / jnp.sqrt(1.0 + sigma * sigma)
    base = state + (0.6 * sigma_of(first + 1.0)[:1]) * noise[pl.ds(0, ROWS, stride=2), :]
    base_out[...] = base
    late_out[...] = (0.6 * sigma_of(second + 1.0)[:1]) * noise[pl.ds(1, ROWS, stride=2), :]
    out[:, 32:48, :] = scaled.reshape(FRAMES, POS, C).astype(BF16)
    out[:, 48:64, :] = base.reshape(FRAMES, POS, C).astype(BF16)
    row = iota((3 * HDIM, 1), 0)
    target = (row % HDIM) // PART * HDIM + row // HDIM * PART + row % PART
    pick = (iota((3 * HDIM, 4 * HDIM), 1) == target).astype(F32).astype(BF16)
    stacked = jnp.concatenate(
        [
            jnp.concatenate(
                [w_qkv[:, s * D + h * HDIM : s * D + (h + 1) * HDIM] for s in range(3)], axis=1
            )
            for h in range(HEADS)
        ],
        axis=0,
    )
    pieces = dot(stacked, pick)
    lane = iota((PART, HDIM), 1)
    for h in range(HEADS):
        for i in range(4):
            piece = pieces[h * PART : (h + 1) * PART, i * HDIM : (i + 1) * HDIM]
            piece = jnp.where(lane == 96, first[:1], jnp.where(lane == 97, second[:1], piece))
            out[4 * h + i, 0:32, :] = piece.astype(BF16)


def table_kernel(feats, w_level, w_in, gain, high, low, embed_in):
    emb = dot(feats[...], w_level[...])
    emb_high = emb.astype(BF16)
    embed_in[0:128, :] = w_in[...]
    embed_in[128:160, :] = emb_high
    embed_in[160:192, :] = (emb - emb_high.astype(F32)).astype(BF16)
    embed_in[192:256, :] = jnp.zeros((64, D), BF16)
    scaled = jnp.concatenate([w_in[...].astype(F32), emb], axis=0) * gain[...]
    top = scaled.astype(BF16)
    high[...] = top
    low[...] = (scaled - top.astype(F32)).astype(BF16)


def project_kernel(received, high, low, out):
    part = received[:, 0:32, :].reshape(D, HDIM)
    product = dot(high[...], part) + dot(low[...], part)
    emb = product[128:160]
    beside = jnp.concatenate(
        [pltpu.roll(emb, 96, 1), pltpu.roll(emb, 64, 1), pltpu.roll(emb, 32, 1), jnp.zeros_like(emb)],
        axis=0,
    )
    packed = jnp.where(iota((C, HDIM), 1) < 96, product[:128], beside).astype(BF16)
    out[...] = jnp.broadcast_to(packed[None], out.shape)


def passes_kernel(
    place, reach, received, mine, other, embed_in, gain, w_out, w_res, fresh, out, proj, attn
):
    core = place[0] % 2
    row = iota((4 * HDIM, 1), 0)
    piece = row // HDIM
    target = row % HDIM // PART * HDIM + (piece + core - 2 * (piece % 2) * core) * PART + row % PART
    pick = (iota((4 * HDIM, 4 * HDIM), 1) == target).astype(F32).astype(BF16)
    for h in range(HEADS):
        pieces = jnp.concatenate(
            [mine[2 * h], other[2 * h], mine[2 * h + 1], other[2 * h + 1]], axis=1
        )
        sorted_ = dot(pieces, pick).astype(BF16)
        proj[h, 0:128, :] = sorted_[:, : 3 * HDIM]
        for s in range(3):
            proj[h, 128:160, s * HDIM : (s + 1) * HDIM] = sorted_[
                s * PART : (s + 1) * PART, 3 * HDIM :
            ]
        proj[h, 160:256, :] = jnp.zeros((96, 3 * HDIM), BF16)

    query = iota((SPAN, SPAN), 0)
    key = iota((SPAN, SPAN), 1)
    back = jnp.concatenate([jnp.full((GROUP, SPAN), reach[j], jnp.int32) for j in range(FRAMES)], axis=0)
    allowed = (
        (query % GROUP == key % GROUP)
        & (key // GROUP <= query // GROUP)
        & (key // GROUP >= query // GROUP - back)
    )
    mask = jnp.where(allowed, F32(0.0), F32(-1e30))

    lane = iota((SPAN, HDIM), 1).astype(F32)
    sel_row = iota((HDIM, HDIM), 0)

    def level_at(step):
        sel = (sel_row == 96 + step).astype(F32).astype(BF16)
        rows = dot(received[:, 0:16, :].reshape(FRAMES * 16, HDIM), sel)
        return rows.reshape(FRAMES, 16, HDIM)[:, :GROUP].reshape(SPAN, HDIM)

    def groups(block):
        block = block.astype(F32)
        return [
            block[:, g * GROUP : (g + 1) * GROUP].reshape(SPAN, C) for g in range(POS // GROUP)
        ]

    def predict(tokens, level):
        hot = ((lane == level) | (lane == level + 32.0)).astype(F32).astype(BF16)
        full = jnp.concatenate(
            [
                jnp.concatenate([t.astype(BF16) for t in tokens], axis=0),
                jnp.concatenate([hot] * len(tokens), axis=0),
            ],
            axis=1,
        )
        hidden = dot(full, embed_in[...])
        scale = lax.rsqrt(jnp.mean(hidden * hidden, axis=-1, keepdims=True) + 1e-06)
        normed = (hidden * scale * gain[...]).astype(BF16)
        ones = jnp.ones((SPAN, HDIM), BF16)
        for h in range(HEADS):
            qkv = dot(full, proj[h]) * scale
            query = (qkv[:, :HDIM] * F32(math.log2(math.e) / math.sqrt(HDIM))).astype(BF16)
            keys = qkv[:, HDIM : 2 * HDIM].astype(BF16)
            values = qkv[:, 2 * HDIM :].astype(BF16)
            for g in range(len(tokens)):
                rows = slice(g * SPAN, (g + 1) * SPAN)
                scores = mask + lax.dot_general(
                    query[rows], keys[rows], (((1,), (1,)), ((), ())), preferred_element_type=F32
                )
                expo = jnp.exp2(scores - jnp.max(scores, axis=-1, keepdims=True)).astype(BF16)
                total = dot(expo, jnp.concatenate([values[rows], ones], axis=1))
                attn[rows, h * HDIM : (h + 1) * HDIM] = (
                    total[:, :HDIM] / total[:, HDIM:]
                ).astype(BF16)
        pred = dot(normed, w_res[...]) + dot(attn[...], w_out[...])
        return [pred[g * SPAN : (g + 1) * SPAN] for g in range(len(tokens))]

    first, second = level_at(0), level_at(1)
    share = [0.8 * sigma_of(l + 1.0) - sigma_of(l) for l in (first, second)]
    sigma = sigma_of(second)
    norm = jnp.sqrt(1.0 + sigma * sigma)
    preds = predict(groups(received[:, 32:48, :]), first)
    moved = [share[0] * p for p in preds]
    entering = fresh[pl.ds(pl.multiple_of(place[0] * POS, POS), POS), :]
    tokens = []
    for g, base in enumerate(groups(received[:, 48:64, :])):
        state = jnp.concatenate(
            [(base + moved[g])[GROUP:], entering[g * GROUP : (g + 1) * GROUP]], axis=0
        )
        tokens.append(state / norm)
    preds = predict(tokens, second)
    for g in range(POS // GROUP):
        kept = jnp.concatenate([moved[g][GROUP:], jnp.zeros((GROUP, C), F32)], axis=0)
        preds[g] = (kept + share[1] * preds[g]).reshape(FRAMES, 1, GROUP, C)
    out[...] = jnp.concatenate(preds, axis=1).reshape(FRAMES, POS, C).astype(BF16)


def shifted(block, axis, distance):
    devices = range(lax.axis_size(axis))
    route = [(i - distance, i) for i in devices if i - distance in devices]
    return lax.ppermute(block, axis, route)


def struct(shape, dtype):
    return jax.ShapeDtypeStruct(shape, dtype)


LIMIT = pltpu.CompilerParams(vmem_limit_bytes=40 * 1024 * 1024)


def on_device(window, noise, fresh, levels, reach, w_in, w_level, norm_gain, w_qkv, w_out, w_res):
    place = lax.axis_index("frame")
    gain = norm_gain.reshape(1, D)
    payload, base, late = pl.pallas_call(
        pack_kernel,
        out_shape=(
            struct((FRAMES, 64, C), BF16),
            struct((ROWS, C), F32),
            struct((ROWS, C), F32),
        ),
        in_specs=[SMEM, VMEM, VMEM, VMEM],
        out_specs=(VMEM, VMEM, VMEM),
        compiler_params=LIMIT,
        name="pack",
    )(levels, window, noise.reshape(2 * ROWS, C), w_qkv)
    received = lax.all_to_all(payload, "frame", split_axis=0, concat_axis=0, tiled=True)
    high, low, embed_in = pl.pallas_call(
        table_kernel,
        out_shape=(struct((160, D), BF16), struct((160, D), BF16), struct((256, D), BF16)),
        in_specs=[VMEM] * 4,
        out_specs=(VMEM,) * 3,
        compiler_params=LIMIT,
        name="tables",
    )(feats_table(), w_level, w_in, gain)
    packed = pl.pallas_call(
        project_kernel,
        out_shape=struct((FRAMES // 2, C, HDIM), BF16),
        in_specs=[VMEM] * 3,
        out_specs=VMEM,
        compiler_params=LIMIT,
        name="project",
    )(received, high, low)
    same_core = [list(range(core, FRAMES, 2)) for core in range(2)]
    mine = lax.all_to_all(
        packed, "frame", split_axis=0, concat_axis=0, tiled=True, axis_index_groups=same_core
    )
    other = lax.ppermute(mine, "frame", [(i, i ^ 1) for i in range(FRAMES)])
    delta = pl.pallas_call(
        passes_kernel,
        out_shape=struct((FRAMES, POS, C), BF16),
        in_specs=[SMEM, SMEM] + [VMEM] * 8,
        out_specs=VMEM,
        scratch_shapes=[
            pltpu.VMEM((HEADS, 256, 3 * HDIM), BF16),
            pltpu.VMEM((ROWS, HEADS * HDIM), BF16),
        ],
        compiler_params=LIMIT,
        name="passes",
    )(place.reshape(1), reach, received, mine, other, embed_in, gain, w_out, w_res, fresh)
    back = lax.all_to_all(delta, "frame", split_axis=0, concat_axis=0, tiled=True)
    moved = shifted(base, "frame", -1)
    start = jnp.where(place == FRAMES - 1, fresh, moved)
    return start + late + back.reshape(ROWS, C).astype(F32)


def solution(mesh):
    return jax.shard_map(
        on_device,
        mesh=mesh,
        in_specs=(
            P(("batch", "frame"), None),
            P(("batch", "frame"), None, None),
            P("batch", None),
            P(("batch", "frame"), None),
            P("batch"),
            P(),
            P(),
            P(),
            P("frame", None),
            P(),
            P(),
        ),
        out_specs=P(("batch", "frame"), None),
        check_vma=False,
    )
```

```python
import math

import jax
import jax.numpy as jnp
import numpy as np
from jax import lax
from jax.experimental import pallas as pl
from jax.experimental.pallas import tpu as pltpu
from jax.sharding import PartitionSpec as P

HEADS = 8
HDIM = 128
C = 128
D = 1024
FREQ = 128
LEVELS = 32
FRAMES = 32
ROWS = 512
POS = ROWS // FRAMES
GROUP = 8
SPAN = FRAMES * GROUP
PART = 32
DECAY = math.log(1.0 / 16.0) / LEVELS
BF16 = jnp.bfloat16
F32 = jnp.float32
VMEM = pl.BlockSpec(memory_space=pltpu.VMEM)
SMEM = pl.BlockSpec(memory_space=pltpu.SMEM)
HBM = pl.BlockSpec(memory_space=pltpu.HBM)


def sigma_of(level):
    return 4.0 * jnp.exp(level * F32(DECAY))


def feats_table():
    sigma = 4.0 * np.exp(np.arange(LEVELS) * DECAY)
    freqs = np.exp(np.arange(FREQ) * (math.log(100.0) / FREQ))
    angle = np.log(sigma)[:, None] * freqs[None, :]
    return jnp.asarray(np.concatenate([np.sin(angle), np.cos(angle)], axis=1), F32).astype(BF16)


def dot(a, b):
    return jnp.dot(a, b, preferred_element_type=F32)


def iota(shape, dim):
    return lax.broadcasted_iota(jnp.int32, shape, dim)


def pack_kernel(levels, window_in, noise_in, w_qkv_in, out, base_out, window, noise, w_qkv, sems):
    copies = [
        pltpu.make_async_copy(src, dst, sems.at[k])
        for k, (src, dst) in enumerate(
            [(w_qkv_in, w_qkv), (window_in, window), (noise_in, noise)]
        )
    ]
    for copy in copies:
        copy.start()
    first = jnp.full((8, C), levels[0, 0], jnp.int32).astype(F32)
    second = jnp.full((8, C), levels[0, 1], jnp.int32).astype(F32)
    row = iota((3 * HDIM, 1), 0)
    target = (row % HDIM) // PART * HDIM + row // HDIM * PART + row % PART
    pick = (iota((3 * HDIM, 4 * HDIM), 1) == target).astype(F32).astype(BF16)
    lane = iota((PART, HDIM), 1)
    sigma = sigma_of(first)[:1]
    odd = lax.axis_index("batch") % 2
    copies[0].wait()
    stacked = jnp.concatenate(
        [
            jnp.concatenate(
                [
                    w_qkv[:, pl.ds(pl.multiple_of((s * HEADS + 2 * x + odd) * HDIM, HDIM), HDIM)]
                    for s in range(3)
                ],
                axis=1,
            )
            for x in range(4)
        ],
        axis=0,
    )
    pieces = dot(stacked, pick)
    for x in range(4):
        for i in range(4):
            piece = pieces[x * PART : (x + 1) * PART, i * HDIM : (i + 1) * HDIM]
            piece = jnp.where(lane == 96, first[:1], jnp.where(lane == 97, second[:1], piece))
            piece = piece.astype(BF16)
            out[x * 8 + i, 0:32, :] = piece
            out[x * 8 + i + 4, 0:32, :] = piece
    copies[1].wait()
    state = window[...]
    scaled = state / jnp.sqrt(1.0 + sigma * sigma)
    out[:, 32:48, :] = scaled.reshape(FRAMES, POS, C).astype(BF16)
    copies[2].wait()
    base = state + (0.6 * sigma_of(first + 1.0)[:1]) * noise[pl.ds(0, ROWS, stride=2), :]
    base_out[...] = base
    out[:, 48:64, :] = base.reshape(FRAMES, POS, C).astype(BF16)


def split(value):
    high = value.astype(BF16)
    return high, (value - high.astype(F32)).astype(BF16)


def table_kernel(feats, w_level, w_in, gain, w_res, high, low, embed_in, residual):
    emb = dot(feats[...], w_level[...])
    embed_in[0:128, :] = w_in[...]
    embed_in[128:160, :], embed_in[160:192, :] = split(emb)
    embed_in[192:256, :] = jnp.zeros((64, D), BF16)
    scaled = jnp.concatenate([w_in[...].astype(F32), emb], axis=0) * gain[...]
    high[...], low[...] = split(scaled)
    residual[...] = jnp.zeros((512, C), BF16)
    product = dot(high[...], w_res[...]) + dot(low[...], w_res[...])
    residual[0:160, :], residual[256:416, :] = split(product)


def project_kernel(received, high, low, out):
    part = received[:, 0:32, :].reshape(D, HDIM)
    lane = iota((C, HDIM), 1)
    product = dot(high[...], part) + dot(low[...], part)
    product *= jnp.where(lane[:1] < PART, F32(math.log2(math.e) / math.sqrt(HDIM)), F32(1.0))
    emb = product[128:160]
    beside = jnp.concatenate(
        [pltpu.roll(emb, 96, 1), pltpu.roll(emb, 64, 1), pltpu.roll(emb, 32, 1), jnp.zeros_like(emb)],
        axis=0,
    )
    packed = jnp.where(lane < 96, product[:128], beside).astype(BF16)
    out[...] = jnp.broadcast_to(packed[None], out.shape)


def normalised(tokens, hot, embed_in, residual):
    full = jnp.concatenate([tokens.astype(BF16), hot], axis=1)
    hidden = dot(full, embed_in[...])
    scale = lax.rsqrt(jnp.mean(hidden * hidden, axis=-1, keepdims=True) + 1e-06)
    scale = jnp.broadcast_to(scale, (ROWS, C))
    kept = scale * (dot(full, residual[0:256, :]) + dot(full, residual[256:512, :]))
    halves = [(full[:, k * C : (k + 1) * C].astype(F32) * scale).astype(BF16) for k in range(2)]
    return jnp.concatenate(halves, axis=1), kept


def groups_of(block):
    block = block.astype(F32)
    return jnp.concatenate(
        [block[:, g * GROUP : (g + 1) * GROUP].reshape(SPAN, C) for g in range(POS // GROUP)],
        axis=0,
    )


def before_kernel(
    levels, reach, received, embed_in, residual, fresh, moved, noise, w_out_in,
    normed, kept, base, hot, scales, mask, entering, w_out, start,
):
    place = lax.axis_index("frame")
    last = jnp.full((8, C), place, jnp.int32)[:1] == FRAMES - 1
    level = jnp.full((8, C), levels[0, 1], jnp.int32).astype(F32)[:1]
    late = (0.6 * sigma_of(level + 1.0)) * noise[pl.ds(1, ROWS, stride=2), :]
    start[...] = jnp.where(last, fresh[...], moved[...]) + late
    w_out[...] = w_out_in[...]
    entering[...] = fresh[pl.ds(pl.multiple_of(place * POS, POS), POS), :]
    query = iota((SPAN, SPAN), 0)
    key = iota((SPAN, SPAN), 1)
    back = jnp.concatenate([jnp.full((GROUP, SPAN), reach[j], jnp.int32) for j in range(FRAMES)], axis=0)
    allowed = (
        (query % GROUP == key % GROUP)
        & (key // GROUP <= query // GROUP)
        & (key // GROUP >= query // GROUP - back)
    )
    mask[...] = jnp.where(allowed, F32(0.0), F32(-1e30))
    lane = iota((SPAN, HDIM), 1).astype(F32)
    sel_row = iota((HDIM, HDIM), 0)
    hots = []
    for step in range(2):
        sel = (sel_row == 96 + step).astype(F32).astype(BF16)
        rows = dot(received[:, 0:16, :].reshape(FRAMES * 16, HDIM), sel)
        level = rows.reshape(FRAMES, 16, HDIM)[:, :GROUP].reshape(SPAN, HDIM)
        sigma = sigma_of(level)
        scales[step] = 0.8 * sigma_of(level + 1.0) - sigma
        if step:
            scales[2] = 1.0 / jnp.sqrt(1.0 + sigma * sigma)
        hots.append(((lane == level) | (lane == level + 32.0)).astype(F32).astype(BF16))
    hot[...] = hots[1]
    tokens = groups_of(received[:, 32:48, :])
    base[...] = groups_of(received[:, 48:64, :])
    normed[...], kept[...] = normalised(
        tokens, jnp.concatenate([hots[0], hots[0]], axis=0), embed_in, residual
    )


def passes_kernel(
    mine, other, embed_in, residual, normed, kept, base, hot, scales, mask, entering, w_out,
    out, pairs, values, attn,
):
    core = lax.axis_index("frame") % 2
    row = iota((4 * HDIM, 1), 0)
    piece = row // HDIM
    target = row % HDIM // PART * HDIM + (piece + core - 2 * (piece % 2) * core) * PART + row % PART
    pick = (iota((4 * HDIM, 4 * HDIM), 1) == target).astype(F32).astype(BF16)
    for h in range(HEADS):
        pieces = jnp.concatenate(
            [mine[2 * h], other[2 * h], mine[2 * h + 1], other[2 * h + 1]], axis=1
        )
        ordered = dot(pieces, pick).astype(BF16)
        beside = slice(h % 2 * HDIM, (h % 2 + 1) * HDIM)
        pairs[h, 0:128, :] = ordered[:, : 2 * HDIM]
        values[h // 2, 0:128, beside] = ordered[:, 2 * HDIM : 3 * HDIM]
        pairs[h, 128:160, :HDIM] = ordered[0:32, 3 * HDIM :]
        pairs[h, 128:160, HDIM:] = ordered[32:64, 3 * HDIM :]
        values[h // 2, 128:160, beside] = ordered[64:96, 3 * HDIM :]
        pairs[h, 160:256, :] = jnp.zeros((96, 2 * HDIM), BF16)
        values[h // 2, 160:256, beside] = jnp.zeros((96, HDIM), BF16)
    ones = jnp.ones((SPAN, HDIM), BF16)

    def predict(normed, kept):
        for h in range(HEADS):
            query_key = dot(normed, pairs[h]).astype(BF16)
            if h % 2 == 0:
                both = dot(normed, values[h // 2]).astype(BF16)
            for g in range(POS // GROUP):
                rows = slice(g * SPAN, (g + 1) * SPAN)
                scores = mask[...] + lax.dot_general(
                    query_key[rows, :HDIM],
                    query_key[rows, HDIM:],
                    (((1,), (1,)), ((), ())),
                    preferred_element_type=F32,
                )
                expo = jnp.exp2(scores - jnp.max(scores, axis=-1, keepdims=True)).astype(BF16)
                value = both[rows, h % 2 * HDIM : (h % 2 + 1) * HDIM]
                total = dot(expo, jnp.concatenate([value, ones], axis=1))
                attn[rows, h * HDIM : (h + 1) * HDIM] = (
                    total[:, :HDIM] / total[:, HDIM:]
                ).astype(BF16)
        return kept + dot(attn[...], w_out[...])

    def both_groups(block):
        return jnp.concatenate([block] * (POS // GROUP), axis=0)

    def next_slot(block, entering):
        parts = []
        for g in range(POS // GROUP):
            parts += [block[g * SPAN + GROUP : (g + 1) * SPAN], entering[g * GROUP : (g + 1) * GROUP]]
        return jnp.concatenate(parts, axis=0)

    moved = both_groups(scales[0]) * predict(normed[...], kept[...])
    tokens = next_slot(base[...] + moved, entering[...]) * both_groups(scales[2])
    delta = both_groups(scales[1]) * predict(
        *normalised(tokens, both_groups(hot[...]), embed_in, residual)
    )
    delta += next_slot(moved, jnp.zeros((POS, C), F32))
    parts = [
        delta[g * SPAN : (g + 1) * SPAN].reshape(FRAMES, 1, GROUP, C) for g in range(POS // GROUP)
    ]
    out[...] = jnp.concatenate(parts, axis=1).reshape(FRAMES, POS, C).astype(BF16)


def shifted(block, axis, distance):
    devices = range(lax.axis_size(axis))
    route = [(i - distance, i) for i in devices if i - distance in devices]
    return lax.ppermute(block, axis, route)


def struct(shape, dtype):
    return jax.ShapeDtypeStruct(shape, dtype)


LIMIT = 40 * 1024 * 1024


def spread_groups(batches):
    across = min(batches, 8)
    deep = batches // across * 4

    def index(x, y, z, core):
        return (x * 8 + z % 4 * 2 + core) * batches + z // 4 * across + y

    def pairs(length):
        return [(k, k + 1) for k in range(0, length, 2)]

    return [
        [index(x, y, z, core) for x in range(4) for y in ys for z in zs]
        for core in range(2)
        for ys in pairs(across)
        for zs in pairs(deep)
    ]


def call(kernel, name, out_shape, in_specs, cost, scratch_shapes=(), limit=LIMIT):
    flops, bytes_accessed = cost
    return pl.pallas_call(
        kernel,
        out_shape=out_shape,
        in_specs=in_specs,
        out_specs=jax.tree.map(lambda _: VMEM, out_shape),
        scratch_shapes=scratch_shapes,
        compiler_params=pltpu.CompilerParams(vmem_limit_bytes=limit),
        cost_estimate=pl.CostEstimate(
            flops=flops, bytes_accessed=bytes_accessed, transcendentals=0
        ),
        name=name,
    )


def on_device(window, noise, fresh, levels, reach, w_in, w_level, norm_gain, w_qkv, w_out, w_res):
    pairs_of_noise = noise.reshape(2 * ROWS, C)
    payload, base = call(
        pack_kernel,
        "pack",
        (struct((FRAMES, 64, C), BF16), struct((ROWS, C), F32)),
        [SMEM] + [HBM] * 3,
        (10**8, 2 * 10**6),
        [
            pltpu.VMEM((ROWS, C), F32),
            pltpu.VMEM((2 * ROWS, C), F32),
            pltpu.VMEM((D // FRAMES, 3 * D), BF16),
            pltpu.SemaphoreType.DMA((3,)),
        ],
        None,
    )(levels, window, pairs_of_noise, w_qkv)
    received = lax.all_to_all(payload, "frame", split_axis=0, concat_axis=0, tiled=True)
    moved = shifted(base, "frame", -1)
    moved, w_level = lax.optimization_barrier((moved, w_level))
    high, low, embed_in, residual = call(
        table_kernel,
        "tables",
        (
            struct((160, D), BF16),
            struct((160, D), BF16),
            struct((256, D), BF16),
            struct((512, C), BF16),
        ),
        [VMEM] * 5,
        (10**8, 3 * 10**6),
    )(feats_table(), w_level, w_in, norm_gain.reshape(1, D), w_res)
    packed = call(
        project_kernel,
        "project",
        struct((FRAMES // 2, C, HDIM), BF16),
        [VMEM] * 3,
        (10**8, 2 * 10**6),
    )(received, high, low)
    mine = lax.all_to_all(
        packed,
        ("frame", "batch"),
        split_axis=0,
        concat_axis=0,
        tiled=True,
        axis_index_groups=spread_groups(lax.axis_size("batch")),
    )
    *prepared, start = call(
        before_kernel,
        "before",
        (
            struct((ROWS, 2 * C), BF16),
            struct((ROWS, C), F32),
            struct((ROWS, C), F32),
            struct((SPAN, C), BF16),
            struct((3, SPAN, C), F32),
            struct((SPAN, SPAN), F32),
            struct((POS, C), F32),
            struct((D, C), BF16),
            struct((ROWS, C), F32),
        ),
        [SMEM, SMEM] + [VMEM] * 7,
        (4 * 10**8, 4 * 10**6),
    )(levels, reach, received, embed_in, residual, fresh, moved, pairs_of_noise, w_out)
    other = lax.ppermute(mine, "frame", [(i, i ^ 1) for i in range(FRAMES)])
    delta = call(
        passes_kernel,
        "passes",
        struct((FRAMES, POS, C), BF16),
        [VMEM] * 12,
        (5 * 10**9, 4 * 10**6),
        [
            pltpu.VMEM((HEADS, 256, 2 * HDIM), BF16),
            pltpu.VMEM((HEADS // 2, 256, 2 * HDIM), BF16),
            pltpu.VMEM((ROWS, HEADS * HDIM), BF16),
        ],
    )(mine, other, embed_in, residual, *prepared)
    back = lax.all_to_all(delta, "frame", split_axis=0, concat_axis=0, tiled=True)
    return start + back.reshape(ROWS, C).astype(F32)


def solution(mesh):
    return jax.shard_map(
        on_device,
        mesh=mesh,
        in_specs=(
            P(("batch", "frame"), None),
            P(("batch", "frame"), None, None),
            P("batch", None),
            P(("batch", "frame"), None),
            P("batch"),
            P(),
            P(),
            P(),
            P("frame", None),
            P(),
            P(),
        ),
        out_specs=P(("batch", "frame"), None),
        check_vma=False,
    )
```

```python
import math

import jax
import jax.numpy as jnp
import numpy as np
from jax import lax
from jax.experimental import pallas as pl
from jax.experimental.pallas import tpu as pltpu
from jax.sharding import PartitionSpec as P

HEADS = 8
HDIM = 128
C = 128
D = 1024
FREQ = 128
LEVELS = 32
FRAMES = 32
ROWS = 512
POS = ROWS // FRAMES
GROUP = 8
SPAN = FRAMES * GROUP
PART = 32
DECAY = math.log(1.0 / 16.0) / LEVELS
BF16 = jnp.bfloat16
F32 = jnp.float32
VMEM = pl.BlockSpec(memory_space=pltpu.VMEM)
SMEM = pl.BlockSpec(memory_space=pltpu.SMEM)
HBM = pl.BlockSpec(memory_space=pltpu.HBM)


def sigma_of(level):
    return 4.0 * jnp.exp(level * F32(DECAY))


def feats_table():
    sigma = 4.0 * np.exp(np.arange(LEVELS) * DECAY)
    freqs = np.exp(np.arange(FREQ) * (math.log(100.0) / FREQ))
    angle = np.log(sigma)[:, None] * freqs[None, :]
    return jnp.asarray(np.concatenate([np.sin(angle), np.cos(angle)], axis=1), F32).astype(BF16)


def dot(a, b):
    return jnp.dot(a, b, preferred_element_type=F32)


def iota(shape, dim):
    return lax.broadcasted_iota(jnp.int32, shape, dim)


def pack_kernel(levels, window_in, noise_in, w_qkv_in, out, window, noise, w_qkv, sems):
    copies = [
        pltpu.make_async_copy(src, dst, sems.at[k])
        for k, (src, dst) in enumerate(
            [(w_qkv_in, w_qkv), (window_in, window), (noise_in, noise)]
        )
    ]
    for copy in copies:
        copy.start()
    first = jnp.full((8, C), levels[0, 0], jnp.int32).astype(F32)
    second = jnp.full((8, C), levels[0, 1], jnp.int32).astype(F32)
    row = iota((3 * HDIM, 1), 0)
    target = (row % HDIM) // PART * HDIM + row // HDIM * PART + row % PART
    pick = (iota((3 * HDIM, 4 * HDIM), 1) == target).astype(F32).astype(BF16)
    lane = iota((PART, HDIM), 1)
    sigma = sigma_of(first)[:1]
    odd = lax.axis_index("batch") % 2
    copies[0].wait()
    stacked = jnp.concatenate(
        [
            jnp.concatenate(
                [
                    w_qkv[:, pl.ds(pl.multiple_of((s * HEADS + 2 * x + odd) * HDIM, HDIM), HDIM)]
                    for s in range(3)
                ],
                axis=1,
            )
            for x in range(4)
        ],
        axis=0,
    )
    pieces = dot(stacked, pick)
    for x in range(4):
        for i in range(4):
            piece = pieces[x * PART : (x + 1) * PART, i * HDIM : (i + 1) * HDIM]
            piece = jnp.where(lane == 96, first[:1], jnp.where(lane == 97, second[:1], piece))
            piece = piece.astype(BF16)
            out[x * 8 + i, 0:32, :] = piece
            out[x * 8 + i + 4, 0:32, :] = piece
    copies[1].wait()
    state = window[...]
    scaled = state / jnp.sqrt(1.0 + sigma * sigma)
    out[:, 32:48, :] = scaled.reshape(FRAMES, POS, C).astype(BF16)
    copies[2].wait()
    base = state + (0.6 * sigma_of(first + 1.0)[:1]) * noise[pl.ds(0, ROWS, stride=2), :]
    out[:, 48:64, :] = base.reshape(FRAMES, POS, C).astype(BF16)


def split(value):
    high = value.astype(BF16)
    return high, (value - high.astype(F32)).astype(BF16)


def table_kernel(
    levels, reach, feats, w_level, w_in, gain, w_res, noise,
    high, low, embed_in, residual, mask, late,
):
    emb = dot(feats[...], w_level[...])
    embed_in[0:128, :] = w_in[...]
    embed_in[128:160, :], embed_in[160:192, :] = split(emb)
    embed_in[192:256, :] = jnp.zeros((64, D), BF16)
    scaled = jnp.concatenate([w_in[...].astype(F32), emb], axis=0) * gain[...]
    high[...], low[...] = split(scaled)
    residual[...] = jnp.zeros((256, 2 * C), BF16)
    product = dot(high[...], w_res[...]) + dot(low[...], w_res[...])
    residual[0:160, :C], residual[0:160, C:] = split(product)
    query = iota((SPAN, SPAN), 0)
    key = iota((SPAN, SPAN), 1)
    back = jnp.concatenate([jnp.full((GROUP, SPAN), reach[j], jnp.int32) for j in range(FRAMES)], axis=0)
    allowed = (
        (query % GROUP == key % GROUP)
        & (key // GROUP <= query // GROUP)
        & (key // GROUP >= query // GROUP - back)
    )
    mask[...] = jnp.where(allowed, F32(0.0), F32(-1e30))
    level = jnp.full((8, C), levels[0, 1], jnp.int32).astype(F32)[:1]
    late[...] = (0.6 * sigma_of(level + 1.0)) * noise[pl.ds(1, ROWS, stride=2), :]


def project_kernel(received, high, low, out):
    part = received[:, 0:32, :].reshape(D, HDIM)
    lane = iota((C, HDIM), 1)
    product = dot(high[...], part) + dot(low[...], part)
    product *= jnp.where(lane[:1] < PART, F32(math.log2(math.e) / math.sqrt(HDIM)), F32(1.0))
    emb = product[128:160]
    beside = jnp.concatenate(
        [pltpu.roll(emb, 96, 1), pltpu.roll(emb, 64, 1), pltpu.roll(emb, 32, 1), jnp.zeros_like(emb)],
        axis=0,
    )
    packed = jnp.where(lane < 96, product[:128], beside).astype(BF16)
    out[...] = jnp.broadcast_to(packed[None], out.shape)


def normalised(tokens, hot, embed_in, residual):
    full = jnp.concatenate([tokens.astype(BF16), hot], axis=1)
    hidden = dot(full, embed_in[...])
    scale = lax.rsqrt(jnp.mean(hidden * hidden, axis=-1, keepdims=True) + 1e-06)
    scale = jnp.broadcast_to(scale, (ROWS, C))
    both = dot(full, residual[...])
    kept = scale * (both[:, :C] + both[:, C:])
    halves = [(full[:, k * C : (k + 1) * C].astype(F32) * scale).astype(BF16) for k in range(2)]
    return jnp.concatenate(halves, axis=1), kept


def groups_of(block):
    block = block.astype(F32)
    return jnp.concatenate(
        [block[:, g * GROUP : (g + 1) * GROUP].reshape(SPAN, C) for g in range(POS // GROUP)],
        axis=0,
    )


def before_kernel(
    received, embed_in, residual, fresh, normed, kept, base, hot, scales, entering
):
    place = lax.axis_index("frame")
    entering[...] = fresh[pl.ds(pl.multiple_of(place * POS, POS), POS), :]
    lane = iota((SPAN, HDIM), 1).astype(F32)
    sel_row = iota((HDIM, HDIM), 0)
    hots = []
    for step in range(2):
        sel = (sel_row == 96 + step).astype(F32).astype(BF16)
        rows = dot(received[:, 0:16, :].reshape(FRAMES * 16, HDIM), sel)
        level = rows.reshape(FRAMES, 16, HDIM)[:, :GROUP].reshape(SPAN, HDIM)
        sigma = sigma_of(level)
        scales[step] = 0.8 * sigma_of(level + 1.0) - sigma
        if step:
            scales[2] = 1.0 / jnp.sqrt(1.0 + sigma * sigma)
        hots.append(((lane == level) | (lane == level + 32.0)).astype(F32).astype(BF16))
    hot[...] = hots[1]
    tokens = groups_of(received[:, 32:48, :])
    base[...] = groups_of(received[:, 48:64, :])
    normed[...], kept[...] = normalised(
        tokens, jnp.concatenate([hots[0], hots[0]], axis=0), embed_in, residual
    )


def passes_kernel(
    mine, other, embed_in, residual, mask, w_out, normed, kept, base, hot, scales, entering,
    out, pairs, values, attn,
):
    core = lax.axis_index("frame") % 2
    row = iota((4 * HDIM, 1), 0)
    piece = row // HDIM
    target = row % HDIM // PART * HDIM + (piece + core - 2 * (piece % 2) * core) * PART + row % PART
    pick = (iota((4 * HDIM, 4 * HDIM), 1) == target).astype(F32).astype(BF16)
    pieces = [[mine[2 * h], other[2 * h], mine[2 * h + 1], other[2 * h + 1]] for h in range(HEADS)]
    pieces = jnp.concatenate([jnp.concatenate(four, axis=1) for four in pieces], axis=0)
    in_order = dot(pieces, pick).astype(BF16)
    for h in range(HEADS):
        ordered = in_order[h * C : (h + 1) * C]
        beside = slice(h % 2 * HDIM, (h % 2 + 1) * HDIM)
        pairs[h, 0:128, :] = ordered[:, : 2 * HDIM]
        values[h // 2, 0:128, beside] = ordered[:, 2 * HDIM : 3 * HDIM]
        pairs[h, 128:160, :HDIM] = ordered[0:32, 3 * HDIM :]
        pairs[h, 128:160, HDIM:] = ordered[32:64, 3 * HDIM :]
        values[h // 2, 128:160, beside] = ordered[64:96, 3 * HDIM :]
        pairs[h, 160:256, :] = jnp.zeros((96, 2 * HDIM), BF16)
        values[h // 2, 160:256, beside] = jnp.zeros((96, HDIM), BF16)
    ones = jnp.ones((SPAN, HDIM), BF16)

    def project(normed, h):
        both = dot(normed, values[h // 2]).astype(BF16) if h % 2 == 0 else None
        return dot(normed, pairs[h]).astype(BF16), both

    def score(query_key, g):
        rows = slice(g * SPAN, (g + 1) * SPAN)
        return mask[...] + lax.dot_general(
            query_key[rows, :HDIM],
            query_key[rows, HDIM:],
            (((1,), (1,)), ((), ())),
            preferred_element_type=F32,
        )

    def soften(scores):
        return jnp.exp2(scores - jnp.max(scores, axis=-1, keepdims=True)).astype(BF16)

    def gather(expo, both, h, g):
        rows = slice(g * SPAN, (g + 1) * SPAN)
        value = both[rows, h % 2 * HDIM : (h % 2 + 1) * HDIM]
        total = dot(expo, jnp.concatenate([value, ones], axis=1))
        attn[rows, h * HDIM : (h + 1) * HDIM] = (total[:, :HDIM] / total[:, HDIM:]).astype(BF16)

    def predict(normed, kept):
        steps = range(POS // GROUP)
        projected, both, scores, expo = {}, {}, {}, {}
        for now in range(HEADS + 3):
            if now < HEADS:
                projected[now], pair = project(normed, now)
                both[now] = both[now - 1] if pair is None else pair
            if 0 <= now - 1 < HEADS:
                scores[now - 1] = [score(projected[now - 1], g) for g in steps]
            if 0 <= now - 2 < HEADS:
                expo[now - 2] = [soften(block) for block in scores[now - 2]]
            if 0 <= now - 3 < HEADS:
                for g in steps:
                    gather(expo[now - 3][g], both[now - 3], now - 3, g)
        return kept + dot(attn[...], w_out[...])

    def both_groups(block):
        return jnp.concatenate([block] * (POS // GROUP), axis=0)

    def next_slot(block):
        parts = []
        for g in range(POS // GROUP):
            parts += [block[g * SPAN + GROUP : (g + 1) * SPAN], entering[g * GROUP : (g + 1) * GROUP]]
        return jnp.concatenate(parts, axis=0)

    state = next_slot(base[...] + both_groups(scales[0]) * predict(normed[...], kept[...]))
    tokens = state * both_groups(scales[2])
    state += both_groups(scales[1]) * predict(
        *normalised(tokens, both_groups(hot[...]), embed_in, residual)
    )
    parts = [
        state[g * SPAN : (g + 1) * SPAN].reshape(FRAMES, 1, GROUP, C) for g in range(POS // GROUP)
    ]
    out[...] = jnp.concatenate(parts, axis=1).reshape(FRAMES, POS, C).astype(BF16)


def struct(shape, dtype):
    return jax.ShapeDtypeStruct(shape, dtype)


LIMIT = 40 * 1024 * 1024


def spread_groups(batches):
    across = min(batches, 8)
    deep = batches // across * 4

    def index(x, y, z, core):
        return (x * 8 + z % 4 * 2 + core) * batches + z // 4 * across + y

    def pairs(length):
        return [(k, k + 1) for k in range(0, length, 2)]

    return [
        [index(x, y, z, core) for x in range(4) for y in ys for z in zs]
        for core in range(2)
        for ys in pairs(across)
        for zs in pairs(deep)
    ]


def call(kernel, name, out_shape, in_specs, cost, scratch_shapes=(), limit=LIMIT):
    flops, bytes_accessed = cost
    return pl.pallas_call(
        kernel,
        out_shape=out_shape,
        in_specs=in_specs,
        out_specs=jax.tree.map(lambda _: VMEM, out_shape),
        scratch_shapes=scratch_shapes,
        compiler_params=pltpu.CompilerParams(vmem_limit_bytes=limit),
        cost_estimate=pl.CostEstimate(
            flops=flops, bytes_accessed=bytes_accessed, transcendentals=0
        ),
        name=name,
    )


def on_device(window, noise, fresh, levels, reach, w_in, w_level, norm_gain, w_qkv, w_out, w_res):
    pairs_of_noise = noise.reshape(2 * ROWS, C)
    payload = call(
        pack_kernel,
        "pack",
        struct((FRAMES, 64, C), BF16),
        [SMEM] + [HBM] * 3,
        (10**8, 2 * 10**6),
        [
            pltpu.VMEM((ROWS, C), F32),
            pltpu.VMEM((2 * ROWS, C), F32),
            pltpu.VMEM((D // FRAMES, 3 * D), BF16),
            pltpu.SemaphoreType.DMA((3,)),
        ],
        None,
    )(levels, window, pairs_of_noise, w_qkv)
    received = lax.all_to_all(payload, "frame", split_axis=0, concat_axis=0, tiled=True)
    high, low, embed_in, residual, mask, late = call(
        table_kernel,
        "tables",
        (
            struct((160, D), BF16),
            struct((160, D), BF16),
            struct((256, D), BF16),
            struct((256, 2 * C), BF16),
            struct((SPAN, SPAN), F32),
            struct((ROWS, C), F32),
        ),
        [SMEM, SMEM] + [VMEM] * 6,
        (10**8, 3 * 10**6),
    )(
        levels, reach, feats_table(), w_level, w_in, norm_gain.reshape(1, D), w_res,
        pairs_of_noise,
    )
    packed = call(
        project_kernel,
        "project",
        struct((FRAMES // 2, C, HDIM), BF16),
        [VMEM] * 3,
        (10**8, 2 * 10**6),
    )(received, high, low)
    mine = lax.all_to_all(
        packed,
        ("frame", "batch"),
        split_axis=0,
        concat_axis=0,
        tiled=True,
        axis_index_groups=spread_groups(lax.axis_size("batch")),
    )
    prepared = call(
        before_kernel,
        "before",
        (
            struct((ROWS, 2 * C), BF16),
            struct((ROWS, C), F32),
            struct((ROWS, C), F32),
            struct((SPAN, C), BF16),
            struct((3, SPAN, C), F32),
            struct((POS, C), F32),
        ),
        [VMEM] * 4,
        (4 * 10**8, 4 * 10**6),
    )(received, embed_in, residual, fresh)
    other = lax.ppermute(mine, "frame", [(i, i ^ 1) for i in range(FRAMES)])
    state = call(
        passes_kernel,
        "passes",
        struct((FRAMES, POS, C), BF16),
        [VMEM] * 12,
        (5 * 10**9, 4 * 10**6),
        [
            pltpu.VMEM((HEADS, 256, 2 * HDIM), BF16),
            pltpu.VMEM((HEADS // 2, 256, 2 * HDIM), BF16),
            pltpu.VMEM((ROWS, HEADS * HDIM), BF16),
        ],
    )(mine, other, embed_in, residual, mask, w_out, *prepared)
    back = lax.all_to_all(state, "frame", split_axis=0, concat_axis=0, tiled=True)
    return late + back.reshape(ROWS, C).astype(F32)


def solution(mesh):
    return jax.shard_map(
        on_device,
        mesh=mesh,
        in_specs=(
            P(("batch", "frame"), None),
            P(("batch", "frame"), None, None),
            P("batch", None),
            P(("batch", "frame"), None),
            P("batch"),
            P(),
            P(),
            P(),
            P("frame", None),
            P(),
            P(),
        ),
        out_specs=P(("batch", "frame"), None),
        check_vma=False,
    )
```

```python
import math

import jax
import jax.numpy as jnp
import numpy as np
from jax import lax
from jax.experimental import pallas as pl
from jax.experimental.pallas import tpu as pltpu
from jax.sharding import PartitionSpec as P

HEADS = 8
HALF = HEADS // 2
HDIM = 128
C = 128
D = 1024
FREQ = 128
LEVELS = 32
FRAMES = 32
ROWS = 512
POS = ROWS // FRAMES
GROUP = 8
SPAN = FRAMES * GROUP
PART = 32
DECAY = math.log(1.0 / 16.0) / LEVELS
BF16 = jnp.bfloat16
F32 = jnp.float32
VMEM = pl.BlockSpec(memory_space=pltpu.VMEM)
SMEM = pl.BlockSpec(memory_space=pltpu.SMEM)
HBM = pl.BlockSpec(memory_space=pltpu.HBM)


def sigma_of(level):
    return 4.0 * jnp.exp(level * F32(DECAY))


def feats_table():
    sigma = 4.0 * np.exp(np.arange(LEVELS) * DECAY)
    freqs = np.exp(np.arange(FREQ) * (math.log(100.0) / FREQ))
    angle = np.log(sigma)[:, None] * freqs[None, :]
    return jnp.asarray(np.concatenate([np.sin(angle), np.cos(angle)], axis=1), F32).astype(BF16)


def dot(a, b):
    return jnp.dot(a, b, preferred_element_type=F32)


def iota(shape, dim):
    return lax.broadcasted_iota(jnp.int32, shape, dim)


def pack_kernel(levels, window_in, noise_in, w_qkv_in, out, window, noise, w_qkv, sems):
    copies = [
        pltpu.make_async_copy(src, dst, sems.at[k])
        for k, (src, dst) in enumerate(
            [(w_qkv_in, w_qkv), (window_in, window), (noise_in, noise)]
        )
    ]
    for copy in copies:
        copy.start()
    first = jnp.full((8, C), levels[0, 0], jnp.int32).astype(F32)
    second = jnp.full((8, C), levels[0, 1], jnp.int32).astype(F32)
    odd = lax.axis_index("batch") % 2
    row = iota((3 * HDIM, 1), 0)
    target = (row % HDIM // PART - 2 * odd) * HDIM + row // HDIM * PART + row % PART
    pick = (iota((3 * HDIM, 2 * HDIM), 1) == target).astype(F32).astype(BF16)
    lane = iota((PART, HDIM), 1)
    sigma = sigma_of(first)[:1]
    copies[0].wait()
    stacked = jnp.concatenate(
        [
            jnp.concatenate(
                [w_qkv[:, s * D + h * HDIM : s * D + (h + 1) * HDIM] for s in range(3)], axis=1
            )
            for h in range(HEADS)
        ],
        axis=0,
    )
    pieces = dot(stacked, pick)
    for h in range(HEADS):
        for i in range(2):
            piece = pieces[h * PART : (h + 1) * PART, i * HDIM : (i + 1) * HDIM]
            piece = jnp.where(lane == 96, first[:1], jnp.where(lane == 97, second[:1], piece))
            piece = piece.astype(BF16)
            for z in (i, i + 2):
                out[h // 2 * 8 + z * 2 + h % 2, 0:32, :] = piece
    copies[1].wait()
    state = window[...]
    scaled = state / jnp.sqrt(1.0 + sigma * sigma)
    out[:, 32:48, :] = scaled.reshape(FRAMES, POS, C).astype(BF16)
    copies[2].wait()
    base = state + (0.6 * sigma_of(first + 1.0)[:1]) * noise[pl.ds(0, ROWS, stride=2), :]
    out[:, 48:64, :] = base.reshape(FRAMES, POS, C).astype(BF16)


def split(value):
    high = value.astype(BF16)
    return high, (value - high.astype(F32)).astype(BF16)


def table_kernel(
    levels, reach, feats, w_level, w_in, gain, w_res, noise,
    high, low, embed_in, residual, mask, late,
):
    emb = dot(feats[...], w_level[...])
    embed_in[0:128, :] = w_in[...]
    embed_in[128:160, :], embed_in[160:192, :] = split(emb)
    embed_in[192:256, :] = jnp.zeros((64, D), BF16)
    scaled = jnp.concatenate([w_in[...].astype(F32), emb], axis=0) * gain[...]
    high[...], low[...] = split(scaled)
    residual[...] = jnp.zeros((256, 2 * C), BF16)
    product = dot(high[...], w_res[...]) + dot(low[...], w_res[...])
    residual[0:160, :C], residual[0:160, C:] = split(product)
    query = iota((SPAN, SPAN), 0)
    key = iota((SPAN, SPAN), 1)
    back = jnp.concatenate([jnp.full((GROUP, SPAN), reach[j], jnp.int32) for j in range(FRAMES)], axis=0)
    allowed = (
        (query % GROUP == key % GROUP)
        & (key // GROUP <= query // GROUP)
        & (key // GROUP >= query // GROUP - back)
    )
    mask[...] = jnp.where(allowed, F32(0.0), F32(-1e30))
    level = jnp.full((8, C), levels[0, 1], jnp.int32).astype(F32)[:1]
    late[...] = (0.6 * sigma_of(level + 1.0)) * noise[pl.ds(1, ROWS, stride=2), :]


def project_kernel(received, high, low, out):
    part = received[:, 0:32, :].reshape(D, HDIM)
    lane = iota((C, HDIM), 1)
    product = dot(high[...], part) + dot(low[...], part)
    product *= jnp.where(lane[:1] < PART, F32(math.log2(math.e) / math.sqrt(HDIM)), F32(1.0))
    emb = product[128:160]
    beside = jnp.concatenate(
        [pltpu.roll(emb, 96, 1), pltpu.roll(emb, 64, 1), pltpu.roll(emb, 32, 1), jnp.zeros_like(emb)],
        axis=0,
    )
    packed = jnp.where(lane < 96, product[:128], beside).astype(BF16)
    out[...] = jnp.broadcast_to(packed[None], out.shape)


def normalised(tokens, hot, embed_in, residual):
    full = jnp.concatenate([tokens.astype(BF16), hot], axis=1)
    hidden = dot(full, embed_in[...])
    scale = lax.rsqrt(jnp.mean(hidden * hidden, axis=-1, keepdims=True) + 1e-06)
    scale = jnp.broadcast_to(scale, (ROWS, C))
    both = dot(full, residual[...])
    kept = scale * (both[:, :C] + both[:, C:])
    halves = [(full[:, k * C : (k + 1) * C].astype(F32) * scale).astype(BF16) for k in range(2)]
    return jnp.concatenate(halves, axis=1), kept


def groups_of(block):
    block = block.astype(F32)
    return jnp.concatenate(
        [block[:, g * GROUP : (g + 1) * GROUP].reshape(SPAN, C) for g in range(POS // GROUP)],
        axis=0,
    )


def sort_columns(held, pairs, values):
    row = iota((4 * HDIM, 1), 0)
    target = row % HDIM // PART * HDIM + row // HDIM * PART + row % PART
    pick = (iota((4 * HDIM, 4 * HDIM), 1) == target).astype(F32).astype(BF16)
    pieces = [jnp.concatenate([held[4 * k + i] for i in range(4)], axis=1) for k in range(HALF)]
    in_order = dot(jnp.concatenate(pieces, axis=0), pick).astype(BF16)
    for k in range(HALF):
        ordered = in_order[k * C : (k + 1) * C]
        beside = slice(k % 2 * HDIM, (k % 2 + 1) * HDIM)
        pairs[k, 0:128, :] = ordered[:, : 2 * HDIM]
        values[k // 2, 0:128, beside] = ordered[:, 2 * HDIM : 3 * HDIM]
        pairs[k, 128:160, :HDIM] = ordered[0:32, 3 * HDIM :]
        pairs[k, 128:160, HDIM:] = ordered[32:64, 3 * HDIM :]
        values[k // 2, 128:160, beside] = ordered[64:96, 3 * HDIM :]
        pairs[k, 160:256, :] = jnp.zeros((96, 2 * HDIM), BF16)
        values[k // 2, 160:256, beside] = jnp.zeros((96, HDIM), BF16)


def project(normed, weights):
    return dot(normed, weights).astype(BF16)


def projected_before(normed, rows):
    return rows


def attend(normed, heads, mask, attn):
    ones = jnp.ones((SPAN, HDIM), BF16)
    groups = [slice(g * SPAN, (g + 1) * SPAN) for g in range(POS // GROUP)]
    projected, both, scores, expo = {}, {}, {}, {}
    for now in range(len(heads) + 3):
        if now < len(heads):
            pairs, values, k, projects = heads[now]
            both[now] = both[now - 1] if k % 2 else projects(normed, values[k // 2])
            projected[now] = projects(normed, pairs[k])
        if 0 <= now - 1 < len(heads):
            scores[now - 1] = [
                mask[...]
                + lax.dot_general(
                    projected[now - 1][rows, :HDIM],
                    projected[now - 1][rows, HDIM:],
                    (((1,), (1,)), ((), ())),
                    preferred_element_type=F32,
                )
                for rows in groups
            ]
        if 0 <= now - 2 < len(heads):
            expo[now - 2] = [
                jnp.exp2(block - jnp.max(block, axis=-1, keepdims=True)).astype(BF16)
                for block in scores[now - 2]
            ]
        if 0 <= now - 3 < len(heads):
            h = now - 3
            for rows, weights in zip(groups, expo[h]):
                value = both[h][rows, h % 2 * HDIM : (h % 2 + 1) * HDIM]
                total = dot(weights, jnp.concatenate([value, ones], axis=1))
                attn[rows, h * HDIM : (h + 1) * HDIM] = (
                    total[:, :HDIM] / total[:, HDIM:]
                ).astype(BF16)


def before_kernel(
    received, mine, embed_in, residual, w_out, fresh,
    normed, kept, base, hot, scales, entering, pairs, values, first_pairs, first_values, w_sorted,
):
    place = lax.axis_index("frame")
    entering[...] = fresh[pl.ds(pl.multiple_of(place * POS, POS), POS), :]
    lane = iota((SPAN, HDIM), 1).astype(F32)
    sel_row = iota((HDIM, HDIM), 0)
    hots = []
    for step in range(2):
        sel = (sel_row == 96 + step).astype(F32).astype(BF16)
        rows = dot(received[:, 0:16, :].reshape(FRAMES * 16, HDIM), sel)
        level = rows.reshape(FRAMES, 16, HDIM)[:, :GROUP].reshape(SPAN, HDIM)
        sigma = sigma_of(level)
        scales[step] = 0.8 * sigma_of(level + 1.0) - sigma
        if step:
            scales[2] = 1.0 / jnp.sqrt(1.0 + sigma * sigma)
        hots.append(((lane == level) | (lane == level + 32.0)).astype(F32).astype(BF16))
    hot[...] = hots[1]
    tokens = groups_of(received[:, 32:48, :])
    base[...] = groups_of(received[:, 48:64, :])
    unit, kept[...] = normalised(
        tokens, jnp.concatenate([hots[0], hots[0]], axis=0), embed_in, residual
    )
    normed[...] = unit
    for k in range(HEADS):
        head = 2 * (k % HALF) + (place + k // HALF) % 2
        rows = pl.ds(pl.multiple_of(head * HDIM, HDIM), HDIM)
        w_sorted[k * HDIM : (k + 1) * HDIM, :] = w_out[rows, :]
    sort_columns(mine, pairs, values)
    for k in range(HALF):
        first_pairs[k] = project(unit, pairs[k])
    for k in range(HALF // 2):
        first_values[k] = project(unit, values[k])


def passes_kernel(
    other, embed_in, residual, mask,
    normed, kept, base, hot, scales, entering, own_pairs, own_values,
    first_pairs, first_values, w_sorted,
    out, pairs, values, attn,
):
    sort_columns(other, pairs, values)
    first = [(first_pairs, first_values, k, projected_before) for k in range(HALF)]
    own = [(own_pairs, own_values, k, project) for k in range(HALF)]
    others = [(pairs, values, k, project) for k in range(HALF)]

    def both_groups(block):
        return jnp.concatenate([block] * (POS // GROUP), axis=0)

    def next_slot(block):
        parts = []
        for g in range(POS // GROUP):
            parts += [block[g * SPAN + GROUP : (g + 1) * SPAN], entering[g * GROUP : (g + 1) * GROUP]]
        return jnp.concatenate(parts, axis=0)

    attend(normed[...], first + others, mask, attn)
    groups = [slice(g * SPAN, (g + 1) * SPAN) for g in range(POS // GROUP)]
    preds = [kept[rows, :] + dot(attn[rows, :], w_sorted[...]) for rows in groups]
    pred = jnp.concatenate(preds, axis=0)
    state = next_slot(base[...] + both_groups(scales[0]) * pred)
    tokens = state * both_groups(scales[2])
    unit, pred = normalised(tokens, both_groups(hot[...]), embed_in, residual)
    attend(unit, own + others, mask, attn)
    state += both_groups(scales[1]) * (pred + dot(attn[...], w_sorted[...]))
    parts = [
        state[g * SPAN : (g + 1) * SPAN].reshape(FRAMES, 1, GROUP, C) for g in range(POS // GROUP)
    ]
    out[...] = jnp.concatenate(parts, axis=1).reshape(FRAMES, POS, C).astype(BF16)


def struct(shape, dtype):
    return jax.ShapeDtypeStruct(shape, dtype)


LIMIT = 40 * 1024 * 1024


def spread_groups(batches):
    across = min(batches, 8)
    deep = batches // across * 4

    def index(x, y, z, core):
        return (x * 8 + z % 4 * 2 + core) * batches + z // 4 * across + y

    def pairs(length):
        return [(k, k + 1) for k in range(0, length, 2)]

    return [
        [index(x, y, z, core) for x in range(4) for y in ys for z in zs]
        for core in range(2)
        for ys in pairs(across)
        for zs in pairs(deep)
    ]


def call(kernel, name, out_shape, in_specs, cost, scratch_shapes=(), limit=LIMIT):
    flops, bytes_accessed = cost
    return pl.pallas_call(
        kernel,
        out_shape=out_shape,
        in_specs=in_specs,
        out_specs=jax.tree.map(lambda _: VMEM, out_shape),
        scratch_shapes=scratch_shapes,
        compiler_params=pltpu.CompilerParams(vmem_limit_bytes=limit),
        cost_estimate=pl.CostEstimate(
            flops=flops, bytes_accessed=bytes_accessed, transcendentals=0
        ),
        name=name,
    )


def on_device(window, noise, fresh, levels, reach, w_in, w_level, norm_gain, w_qkv, w_out, w_res):
    pairs_of_noise = noise.reshape(2 * ROWS, C)
    payload = call(
        pack_kernel,
        "pack",
        struct((FRAMES, 64, C), BF16),
        [SMEM] + [HBM] * 3,
        (10**8, 2 * 10**6),
        [
            pltpu.VMEM((ROWS, C), F32),
            pltpu.VMEM((2 * ROWS, C), F32),
            pltpu.VMEM((D // FRAMES, 3 * D), BF16),
            pltpu.SemaphoreType.DMA((3,)),
        ],
        None,
    )(levels, window, pairs_of_noise, w_qkv)
    received = lax.all_to_all(payload, "frame", split_axis=0, concat_axis=0, tiled=True)
    high, low, embed_in, residual, mask, late = call(
        table_kernel,
        "tables",
        (
            struct((160, D), BF16),
            struct((160, D), BF16),
            struct((256, D), BF16),
            struct((256, 2 * C), BF16),
            struct((SPAN, SPAN), F32),
            struct((ROWS, C), F32),
        ),
        [SMEM, SMEM] + [VMEM] * 6,
        (10**8, 3 * 10**6),
    )(
        levels, reach, feats_table(), w_level, w_in, norm_gain.reshape(1, D), w_res,
        pairs_of_noise,
    )
    packed = call(
        project_kernel,
        "project",
        struct((FRAMES // 2, C, HDIM), BF16),
        [VMEM] * 3,
        (10**8, 2 * 10**6),
    )(received, high, low)
    mine = lax.all_to_all(
        packed,
        ("frame", "batch"),
        split_axis=0,
        concat_axis=0,
        tiled=True,
        axis_index_groups=spread_groups(lax.axis_size("batch")),
    )
    prepared = call(
        before_kernel,
        "before",
        (
            struct((ROWS, 2 * C), BF16),
            struct((ROWS, C), F32),
            struct((ROWS, C), F32),
            struct((SPAN, C), BF16),
            struct((3, SPAN, C), F32),
            struct((POS, C), F32),
            struct((HALF, 256, 2 * HDIM), BF16),
            struct((HALF // 2, 256, 2 * HDIM), BF16),
            struct((HALF, ROWS, 2 * HDIM), BF16),
            struct((HALF // 2, ROWS, 2 * HDIM), BF16),
            struct((D, C), BF16),
        ),
        [VMEM] * 6,
        (10**9, 6 * 10**6),
    )(received, mine, embed_in, residual, w_out, fresh)
    other = lax.ppermute(mine, "frame", [(i, i ^ 1) for i in range(FRAMES)])
    state = call(
        passes_kernel,
        "passes",
        struct((FRAMES, POS, C), BF16),
        [VMEM] * 15,
        (5 * 10**9, 4 * 10**6),
        [
            pltpu.VMEM((HALF, 256, 2 * HDIM), BF16),
            pltpu.VMEM((HALF // 2, 256, 2 * HDIM), BF16),
            pltpu.VMEM((ROWS, HEADS * HDIM), BF16),
        ],
    )(other, embed_in, residual, mask, *prepared)
    back = lax.all_to_all(state, "frame", split_axis=0, concat_axis=0, tiled=True)
    return late + back.reshape(ROWS, C).astype(F32)


def solution(mesh):
    return jax.shard_map(
        on_device,
        mesh=mesh,
        in_specs=(
            P(("batch", "frame"), None),
            P(("batch", "frame"), None, None),
            P("batch", None),
            P(("batch", "frame"), None),
            P("batch"),
            P(),
            P(),
            P(),
            P("frame", None),
            P(),
            P(),
        ),
        out_specs=P(("batch", "frame"), None),
        check_vma=False,
    )
```

```python
import math

import jax
import jax.numpy as jnp
import numpy as np
from jax import lax
from jax.experimental import pallas as pl
from jax.experimental.pallas import tpu as pltpu
from jax.sharding import PartitionSpec as P

HEADS = 8
HALF = HEADS // 2
HDIM = 128
C = 128
D = 1024
FREQ = 128
LEVELS = 32
FRAMES = 32
ROWS = 512
POS = ROWS // FRAMES
GROUP = 8
SPAN = FRAMES * GROUP
PART = 32
DECAY = math.log(1.0 / 16.0) / LEVELS
BF16 = jnp.bfloat16
F32 = jnp.float32
VMEM = pl.BlockSpec(memory_space=pltpu.VMEM)
SMEM = pl.BlockSpec(memory_space=pltpu.SMEM)
HBM = pl.BlockSpec(memory_space=pltpu.HBM)


def sigma_of(level):
    return 4.0 * jnp.exp(level * F32(DECAY))


def feats_table():
    sigma = 4.0 * np.exp(np.arange(LEVELS) * DECAY)
    freqs = np.exp(np.arange(FREQ) * (math.log(100.0) / FREQ))
    angle = np.log(sigma)[:, None] * freqs[None, :]
    return jnp.asarray(np.concatenate([np.sin(angle), np.cos(angle)], axis=1), F32).astype(BF16)


def dot(a, b):
    return jnp.dot(a, b, preferred_element_type=F32)


def iota(shape, dim):
    return lax.broadcasted_iota(jnp.int32, shape, dim)


def pack_kernel(levels, window_in, noise_in, w_qkv_in, out, window, noise, w_qkv, weights, states, sems):
    copies = [
        pltpu.make_async_copy(src, dst, sems.at[k])
        for k, (src, dst) in enumerate(
            [
                (w_qkv_in, w_qkv),
                (window_in, window),
                (noise_in, noise),
                (weights, out.at[:, 0:32]),
                (states.at[0], out.at[:, 32:48]),
                (states.at[1], out.at[:, 48:64]),
            ]
        )
    ]
    for copy in copies[:3]:
        copy.start()
    first = jnp.full((8, C), levels[0, 0], jnp.int32).astype(F32)
    second = jnp.full((8, C), levels[0, 1], jnp.int32).astype(F32)
    odd = lax.axis_index("batch") % 2
    row = iota((3 * HDIM, 1), 0)
    target = (row % HDIM // PART - 2 * odd) * HDIM + row // HDIM * PART + row % PART
    pick = (iota((3 * HDIM, 2 * HDIM), 1) == target).astype(F32).astype(BF16)
    lane = iota((PART, HDIM), 1)
    sigma = sigma_of(first)[:1]
    copies[0].wait()
    stacked = jnp.concatenate(
        [
            jnp.concatenate(
                [w_qkv[:, s * D + h * HDIM : s * D + (h + 1) * HDIM] for s in range(3)], axis=1
            )
            for h in range(HEADS)
        ],
        axis=0,
    )
    pieces = dot(stacked, pick)
    for h in range(HEADS):
        for i in range(2):
            piece = pieces[h * PART : (h + 1) * PART, i * HDIM : (i + 1) * HDIM]
            piece = jnp.where(lane == 96, first[:1], jnp.where(lane == 97, second[:1], piece))
            piece = piece.astype(BF16)
            for z in (i, i + 2):
                weights[h // 2 * 8 + z * 2 + h % 2] = piece
    copies[3].start()
    copies[1].wait()
    state = window[...]
    scaled = state / jnp.sqrt(1.0 + sigma * sigma)
    states[0] = scaled.reshape(FRAMES, POS, C).astype(BF16)
    copies[4].start()
    copies[2].wait()
    base = state + (0.6 * sigma_of(first + 1.0)[:1]) * noise[pl.ds(0, ROWS, stride=2), :]
    states[1] = base.reshape(FRAMES, POS, C).astype(BF16)
    copies[5].start()
    for copy in copies[3:]:
        copy.wait()


def split(value):
    high = value.astype(BF16)
    return high, (value - high.astype(F32)).astype(BF16)


def table_kernel(
    levels, reach, feats, w_level, w_in, gain, w_res, noise,
    high, low, embed_in, residual, mask, late, odd_rows,
):
    emb = dot(feats[...], w_level[...])
    embed_in[0:128, :] = w_in[...]
    embed_in[128:160, :], embed_in[160:192, :] = split(emb)
    embed_in[192:256, :] = jnp.zeros((64, D), BF16)
    scaled = jnp.concatenate([w_in[...].astype(F32), emb], axis=0) * gain[...]
    high[...], low[...] = split(scaled)
    residual[...] = jnp.zeros((256, 2 * C), BF16)
    product = dot(high[...], w_res[...]) + dot(low[...], w_res[...])
    residual[0:160, :C], residual[0:160, C:] = split(product)
    query = iota((SPAN, SPAN), 0)
    key = iota((SPAN, SPAN), 1)
    back = jnp.concatenate([jnp.full((GROUP, SPAN), reach[j], jnp.int32) for j in range(FRAMES)], axis=0)
    allowed = (
        (query % GROUP == key % GROUP)
        & (key // GROUP <= query // GROUP)
        & (key // GROUP >= query // GROUP - back)
    )
    mask[...] = jnp.where(allowed, F32(0.0), F32(-1e30))
    level = jnp.full((8, C), levels[0, 1], jnp.int32).astype(F32)[:1]
    odd_rows[...] = pltpu.roll(noise[...], 2 * ROWS - 1, 0)
    late[...] = (0.6 * sigma_of(level + 1.0)) * odd_rows[pl.ds(0, ROWS, stride=2), :]


def project_kernel(received, high, low, out):
    part = received[:, 0:32, :].reshape(D, HDIM)
    lane = iota((C, HDIM), 1)
    product = dot(high[...], part) + dot(low[...], part)
    product *= jnp.where(lane[:1] < PART, F32(math.log2(math.e) / math.sqrt(HDIM)), F32(1.0))
    emb = product[128:160]
    beside = jnp.concatenate(
        [pltpu.roll(emb, 96, 1), pltpu.roll(emb, 64, 1), pltpu.roll(emb, 32, 1), jnp.zeros_like(emb)],
        axis=0,
    )
    packed = jnp.where(lane < 96, product[:128], beside).astype(BF16)
    out[...] = jnp.broadcast_to(packed[None], out.shape)


def normalised(tokens, hot, embed_in, residual):
    full = jnp.concatenate([tokens.astype(BF16), hot], axis=1)
    hidden = dot(full, embed_in[...])
    scale = lax.rsqrt(jnp.mean(hidden * hidden, axis=-1, keepdims=True) + 1e-06)
    scale = jnp.broadcast_to(scale, (ROWS, C))
    both = dot(full, residual[...])
    kept = scale * (both[:, :C] + both[:, C:])
    halves = [(full[:, k * C : (k + 1) * C].astype(F32) * scale).astype(BF16) for k in range(2)]
    return jnp.concatenate(halves, axis=1), kept


def groups_of(block):
    block = block.astype(F32)
    return jnp.concatenate(
        [block[:, g * GROUP : (g + 1) * GROUP].reshape(SPAN, C) for g in range(POS // GROUP)],
        axis=0,
    )


def sort_columns(held, pairs, values):
    row = iota((4 * HDIM, 1), 0)
    target = row % HDIM // PART * HDIM + row // HDIM * PART + row % PART
    pick = (iota((4 * HDIM, 4 * HDIM), 1) == target).astype(F32).astype(BF16)
    pieces = [jnp.concatenate([held[4 * k + i] for i in range(4)], axis=1) for k in range(HALF)]
    in_order = dot(jnp.concatenate(pieces, axis=0), pick).astype(BF16)
    for k in range(HALF):
        ordered = in_order[k * C : (k + 1) * C]
        beside = slice(k % 2 * HDIM, (k % 2 + 1) * HDIM)
        pairs[k, 0:128, :] = ordered[:, : 2 * HDIM]
        values[k // 2, 0:128, beside] = ordered[:, 2 * HDIM : 3 * HDIM]
        pairs[k, 128:160, :HDIM] = ordered[0:32, 3 * HDIM :]
        pairs[k, 128:160, HDIM:] = ordered[32:64, 3 * HDIM :]
        values[k // 2, 128:160, beside] = ordered[64:96, 3 * HDIM :]
        pairs[k, 160:256, :] = jnp.zeros((96, 2 * HDIM), BF16)
        values[k // 2, 160:256, beside] = jnp.zeros((96, HDIM), BF16)


def project(normed, weights):
    return dot(normed, weights).astype(BF16)


def projected_before(normed, rows):
    return rows


def attend(normed, heads, mask, attn):
    ones = jnp.ones((SPAN, HDIM), BF16)
    groups = [slice(g * SPAN, (g + 1) * SPAN) for g in range(POS // GROUP)]
    projected, both, scores, expo = {}, {}, {}, {}
    for now in range(len(heads) + 3):
        if now < len(heads):
            pairs, values, k, projects = heads[now]
            both[now] = both[now - 1] if k % 2 else projects(normed, values[k // 2])
            projected[now] = projects(normed, pairs[k])
        if 0 <= now - 1 < len(heads):
            scores[now - 1] = [
                mask[...]
                + lax.dot_general(
                    projected[now - 1][rows, :HDIM],
                    projected[now - 1][rows, HDIM:],
                    (((1,), (1,)), ((), ())),
                    preferred_element_type=F32,
                )
                for rows in groups
            ]
        if 0 <= now - 2 < len(heads):
            expo[now - 2] = [
                jnp.exp2(block - jnp.max(block, axis=-1, keepdims=True)).astype(BF16)
                for block in scores[now - 2]
            ]
        if 0 <= now - 3 < len(heads):
            h = now - 3
            for rows, weights in zip(groups, expo[h]):
                value = both[h][rows, h % 2 * HDIM : (h % 2 + 1) * HDIM]
                total = dot(weights, jnp.concatenate([value, ones], axis=1))
                attn[rows, h * HDIM : (h + 1) * HDIM] = (
                    total[:, :HDIM] / total[:, HDIM:]
                ).astype(BF16)


def before_kernel(
    received, mine, embed_in, residual, w_out, fresh,
    normed, kept, base, hot, scales, entering, pairs, values, first_pairs, first_values, w_sorted,
):
    place = lax.axis_index("frame")
    entering[...] = fresh[pl.ds(pl.multiple_of(place * POS, POS), POS), :]
    lane = iota((SPAN, HDIM), 1).astype(F32)
    sel_row = iota((HDIM, HDIM), 0)
    hots = []
    for step in range(2):
        sel = (sel_row == 96 + step).astype(F32).astype(BF16)
        rows = dot(received[:, 0:16, :].reshape(FRAMES * 16, HDIM), sel)
        level = rows.reshape(FRAMES, 16, HDIM)[:, :GROUP].reshape(SPAN, HDIM)
        sigma = sigma_of(level)
        scales[step] = 0.8 * sigma_of(level + 1.0) - sigma
        if step:
            scales[2] = 1.0 / jnp.sqrt(1.0 + sigma * sigma)
        hots.append(((lane == level) | (lane == level + 32.0)).astype(F32).astype(BF16))
    hot[...] = hots[1]
    tokens = groups_of(received[:, 32:48, :])
    base[...] = groups_of(received[:, 48:64, :])
    unit, kept[...] = normalised(
        tokens, jnp.concatenate([hots[0], hots[0]], axis=0), embed_in, residual
    )
    normed[...] = unit
    for k in range(HEADS):
        head = 2 * (k % HALF) + (place + k // HALF) % 2
        rows = pl.ds(pl.multiple_of(head * HDIM, HDIM), HDIM)
        w_sorted[k * HDIM : (k + 1) * HDIM, :] = w_out[rows, :]
    sort_columns(mine, pairs, values)
    for k in range(HALF):
        first_pairs[k] = project(unit, pairs[k])
    for k in range(HALF // 2):
        first_values[k] = project(unit, values[k])


def passes_kernel(
    other, embed_in, residual, mask,
    normed, kept, base, hot, scales, entering, own_pairs, own_values,
    first_pairs, first_values, w_sorted,
    out, pairs, values, attn,
):
    sort_columns(other, pairs, values)
    first = [(first_pairs, first_values, k, projected_before) for k in range(HALF)]
    own = [(own_pairs, own_values, k, project) for k in range(HALF)]
    others = [(pairs, values, k, project) for k in range(HALF)]

    def both_groups(block):
        return jnp.concatenate([block] * (POS // GROUP), axis=0)

    def next_slot(block):
        parts = []
        for g in range(POS // GROUP):
            parts += [block[g * SPAN + GROUP : (g + 1) * SPAN], entering[g * GROUP : (g + 1) * GROUP]]
        return jnp.concatenate(parts, axis=0)

    attend(normed[...], first + others, mask, attn)
    groups = [slice(g * SPAN, (g + 1) * SPAN) for g in range(POS // GROUP)]
    preds = [kept[rows, :] + dot(attn[rows, :], w_sorted[...]) for rows in groups]
    pred = jnp.concatenate(preds, axis=0)
    state = next_slot(base[...] + both_groups(scales[0]) * pred)
    tokens = state * both_groups(scales[2])
    unit, pred = normalised(tokens, both_groups(hot[...]), embed_in, residual)
    attend(unit, own + others, mask, attn)
    state += both_groups(scales[1]) * (pred + dot(attn[...], w_sorted[...]))
    parts = [
        state[g * SPAN : (g + 1) * SPAN].reshape(FRAMES, 1, GROUP, C) for g in range(POS // GROUP)
    ]
    out[...] = jnp.concatenate(parts, axis=1).reshape(FRAMES, POS, C).astype(BF16)


def struct(shape, dtype):
    return jax.ShapeDtypeStruct(shape, dtype)


LIMIT = 40 * 1024 * 1024


def spread_groups(batches):
    across = min(batches, 8)
    deep = batches // across * 4

    def index(x, y, z, core):
        return (x * 8 + z % 4 * 2 + core) * batches + z // 4 * across + y

    def pairs(length):
        return [(k, k + 1) for k in range(0, length, 2)]

    return [
        [index(x, y, z, core) for x in range(4) for y in ys for z in zs]
        for core in range(2)
        for ys in pairs(across)
        for zs in pairs(deep)
    ]


def call(kernel, name, out_shape, in_specs, cost, scratch_shapes=(), limit=LIMIT, outputs=VMEM):
    flops, bytes_accessed = cost
    return pl.pallas_call(
        kernel,
        out_shape=out_shape,
        in_specs=in_specs,
        out_specs=jax.tree.map(lambda _: outputs, out_shape),
        scratch_shapes=scratch_shapes,
        compiler_params=pltpu.CompilerParams(vmem_limit_bytes=limit),
        cost_estimate=pl.CostEstimate(
            flops=flops, bytes_accessed=bytes_accessed, transcendentals=0
        ),
        name=name,
    )


def on_device(window, noise, fresh, levels, reach, w_in, w_level, norm_gain, w_qkv, w_out, w_res):
    pairs_of_noise = noise.reshape(2 * ROWS, C)
    payload = call(
        pack_kernel,
        "pack",
        struct((FRAMES, 64, C), BF16),
        [SMEM] + [HBM] * 3,
        (10**8, 2 * 10**6),
        [
            pltpu.VMEM((ROWS, C), F32),
            pltpu.VMEM((2 * ROWS, C), F32),
            pltpu.VMEM((D // FRAMES, 3 * D), BF16),
            pltpu.VMEM((FRAMES, 32, C), BF16),
            pltpu.VMEM((2, FRAMES, POS, C), BF16),
            pltpu.SemaphoreType.DMA((6,)),
        ],
        None,
        HBM,
    )(levels, window, pairs_of_noise, w_qkv)
    received = lax.all_to_all(payload, "frame", split_axis=0, concat_axis=0, tiled=True)
    high, low, embed_in, residual, mask, late = call(
        table_kernel,
        "tables",
        (
            struct((160, D), BF16),
            struct((160, D), BF16),
            struct((256, D), BF16),
            struct((256, 2 * C), BF16),
            struct((SPAN, SPAN), F32),
            struct((ROWS, C), F32),
        ),
        [SMEM, SMEM] + [VMEM] * 6,
        (10**8, 3 * 10**6),
        [pltpu.VMEM((2 * ROWS, C), F32)],
    )(
        levels, reach, feats_table(), w_level, w_in, norm_gain.reshape(1, D), w_res,
        pairs_of_noise,
    )
    packed = call(
        project_kernel,
        "project",
        struct((FRAMES // 2, C, HDIM), BF16),
        [VMEM] * 3,
        (10**8, 2 * 10**6),
    )(received, high, low)
    mine = lax.all_to_all(
        packed,
        ("frame", "batch"),
        split_axis=0,
        concat_axis=0,
        tiled=True,
        axis_index_groups=spread_groups(lax.axis_size("batch")),
    )
    prepared = call(
        before_kernel,
        "before",
        (
            struct((ROWS, 2 * C), BF16),
            struct((ROWS, C), F32),
            struct((ROWS, C), F32),
            struct((SPAN, C), BF16),
            struct((3, SPAN, C), F32),
            struct((POS, C), F32),
            struct((HALF, 256, 2 * HDIM), BF16),
            struct((HALF // 2, 256, 2 * HDIM), BF16),
            struct((HALF, ROWS, 2 * HDIM), BF16),
            struct((HALF // 2, ROWS, 2 * HDIM), BF16),
            struct((D, C), BF16),
        ),
        [VMEM] * 6,
        (10**9, 6 * 10**6),
    )(received, mine, embed_in, residual, w_out, fresh)
    other = lax.ppermute(mine, "frame", [(i, i ^ 1) for i in range(FRAMES)])
    state = call(
        passes_kernel,
        "passes",
        struct((FRAMES, POS, C), BF16),
        [VMEM] * 15,
        (5 * 10**9, 4 * 10**6),
        [
            pltpu.VMEM((HALF, 256, 2 * HDIM), BF16),
            pltpu.VMEM((HALF // 2, 256, 2 * HDIM), BF16),
            pltpu.VMEM((ROWS, HEADS * HDIM), BF16),
        ],
    )(other, embed_in, residual, mask, *prepared)
    back = lax.all_to_all(state, "frame", split_axis=0, concat_axis=0, tiled=True)
    return late + back.reshape(ROWS, C).astype(F32)


def solution(mesh):
    return jax.shard_map(
        on_device,
        mesh=mesh,
        in_specs=(
            P(("batch", "frame"), None),
            P(("batch", "frame"), None, None),
            P("batch", None),
            P(("batch", "frame"), None),
            P("batch"),
            P(),
            P(),
            P(),
            P("frame", None),
            P(),
            P(),
        ),
        out_specs=P(("batch", "frame"), None),
        check_vma=False,
    )
```
